256 devices in a mesh: seq: 128 (over y, x, z), kmer: 2 (over core).
Axes of the slice: x: 4, y: 4, z: 8, core: 2. Of those that a mesh axis runs over, the one named last changes fastest.
Arguments:
- profiles: bfloat16 [2048, 131072], P(('seq', 'kmer')), may hold values from -6 to 6
- lengths: int32 [131072], P('seq'), may hold values from 64 to 1024
- owners: int32 [2], replicated, may hold values from 0 to 127
- block_mask: int32 [2, 1024, 8], P(None, 'seq'), may hold values 0 or 1
Outputs:
- scores: bfloat16 [131072, 2, 1024], P('seq', None, 'kmer')
The draws below stay inside these ranges and needn't reach their ends.
All inputs are finite; a program needn't handle non-finite values. No bound on the sum of `block_mask` on one device may be relied on, other than what follows from the above.
Results may differ from the reference program's by a relative error of at most 0.001.
Values may be sent and summed in bfloat16 or wider, within the bound.
No kernel may reach another device: no remote copies, remote signals or barrier semaphores. Data moves between devices by JAX's collectives and lax.ppermute only.
A program may use at most 64 MiB of HBM per device.

```python
import jax
import jax.numpy as jnp
from jax import lax

KM = 2048
PANEL = 1024
BLK = 128
SECTIONS = 2
NSEQ = 131072
N_SEQ = 128


def touch_ends(values, own_key, low, top_value):
    longest = values.shape.index(max(values.shape))
    spots = []
    for shift in (0, 1):
        where = [jax.random.randint(jax.random.fold_in(own_key, axis), (), 0, length) for axis, length in enumerate(values.shape)]
        where[longest] = (where[longest] + shift) % values.shape[longest]
        spots.append(tuple(where))
    return values.at[spots[0]].set(low).at[spots[1]].set(top_value)


def block_levels(key, shape, split, least, top_value):
    def one(position, parts):
        steps = jax.random.uniform(jax.random.fold_in(jax.random.fold_in(key, 6), position), (parts,), jnp.float32, least / len(split), top_value / len(split))
        return jnp.repeat(jnp.exp(steps), shape[position] // parts).reshape((-1,) + (1,) * (len(shape) - position - 1))

    gain = one(*split[0])
    for cut in split[1:]:
        gain = gain * one(*cut)
    return gain


def noise(rng, shape, scale, reach, split=(), held_as=jnp.bfloat16):
    result = scale * jax.random.normal(rng, shape, jnp.float32)
    if split:
        result = result * block_levels(rng, shape, split, -0.22, 0.18)
    return jnp.clip(result, -reach, reach).astype(held_as)


def setup_inputs(seed: int = 0) -> dict:
    splits = jax.random.split(jax.random.key(seed), 5)
    profiles = noise(splits[0], (KM, NSEQ), 1.0, 6.0, ((0, 256),))
    lengths = touch_ends(jax.random.randint(splits[1], (NSEQ,), 64, 1025), jax.random.fold_in(splits[1], 1), 64, 1024).astype(jnp.int32)
    owners = jax.random.randint(splits[2], (SECTIONS,), 0, N_SEQ).astype(jnp.int32)
    block_mask = touch_ends((jax.random.randint(splits[3], (SECTIONS, NSEQ // BLK, PANEL // BLK), 0, 5) < 2).astype(jnp.int32), jax.random.fold_in(splits[3], 1), 0, 1)
    return {"profiles": profiles, "lengths": lengths, "owners": owners, "block_mask": block_mask}


def reference(profiles, lengths, owners, block_mask):
    prof = profiles.astype(jnp.float32)
    row_len = lengths.astype(jnp.float32)
    scale = 256.0 / jnp.sqrt(jnp.float32(KM))
    outs = []
    for section in range(SECTIONS):
        start = owners[section].astype(jnp.int32) * PANEL
        panel = lax.dynamic_slice_in_dim(prof, start, PANEL, 1)
        col_len = lax.dynamic_slice_in_dim(row_len, start, PANEL, 0)
        raw = jnp.dot(prof.T, panel, preferred_element_type=jnp.float32)
        mask = jnp.repeat(jnp.repeat(block_mask[section], BLK, axis=0), BLK, axis=1).astype(jnp.float32)
        norm = scale * lax.rsqrt(row_len[:, None] * col_len[None, :])
        outs.append((raw * norm * mask).astype(jnp.bfloat16))
    return jnp.stack(outs, axis=1)
```

```python
import jax
import jax.numpy as jnp
from jax import lax
from jax.experimental import pallas as pl
from jax.experimental.pallas import tpu as pltpu
from jax.sharding import PartitionSpec as P

KM = 2048
PANEL = 1024
BLK = 128
SECTIONS = 2
HALF = PANEL // 2
WIDTH = SECTIONS * HALF
SWAP = [(0, 1), (1, 0)]
NY, NX, NZ = 4, 4, 8
LINES = [[yx * NZ + z for z in range(NZ)] for yx in range(NY * NX)]
FEATURES = 8
RUN = NZ * FEATURES
GROUP = 4 * RUN
LENS = 16
SCALE = 256.0 / KM**0.5
ROWS = 256
VMEM = pl.BlockSpec(memory_space=pltpu.VMEM)
SMEM = pl.BlockSpec(memory_space=pltpu.SMEM)
CONTRACT = (((0,), (0,)), ((), ()))


def params(mebibytes):
    return pltpu.CompilerParams(vmem_limit_bytes=mebibytes << 20)


def number(y, x, z):
    return (y % NY * NX + x % NX) * NZ + z


def shift(value, turn, by):
    pairs = []
    for y in range(NY):
        for x in range(NX):
            for z in range(NZ):
                for core in range(2):
                    to = number(y, x + by, z) if core == turn else number(y + by, x, z)
                    pairs.append((number(y, x, z) * 2 + core, to * 2 + core))
    return lax.ppermute(value, ("seq", "kmer"), pairs)


def swap(value):
    return lax.ppermute(value, "kmer", SWAP)


def piece_kernel(own_ref, place_ref, a_ref, b_ref, c_ref, d_ref, len_ref, out_ref):
    seq = place_ref[0]
    for i, ref in enumerate((a_ref, b_ref, c_ref, d_ref)):
        out_ref[:, :, i * HALF : (i + 1) * HALF] = jnp.broadcast_to(ref[...][None], (NZ, FEATURES, HALF))
    size = len_ref[...].reshape(1, HALF)
    rows = [jnp.where(own_ref[t] == seq, size, 0) for t in range(SECTIONS)]
    for i in range(2):
        parts = []
        for t in range(SECTIONS):
            value = jnp.right_shift(rows[t], 8) if i == 0 else jnp.bitwise_and(rows[t], 255)
            value = value.astype(jnp.float32)
            parts += [value[:, j * BLK : (j + 1) * BLK] for j in range(HALF // BLK)]
        tile = jnp.concatenate(parts, axis=0).astype(jnp.bfloat16)
        at = 2 * WIDTH + i * BLK
        out_ref[:, :, at : at + BLK] = jnp.broadcast_to(tile[None], (NZ, FEATURES, BLK))


def make_piece(owners, place, profiles, lengths):
    def spec(t, other):
        def index(i, own, at):
            return 0, own[t] * 2 + (1 - at[1] if other else at[1])

        return pl.BlockSpec((FEATURES, HALF), index)

    shape = (NZ, FEATURES, 2 * WIDTH + 2 * BLK)
    return pl.pallas_call(
        piece_kernel,
        grid_spec=pltpu.PrefetchScalarGridSpec(
            num_scalar_prefetch=2,
            grid=(1,),
            in_specs=[
                spec(0, False),
                spec(1, False),
                spec(0, True),
                spec(1, True),
                pl.BlockSpec((HALF,), lambda i, own, at: (at[1],)),
            ],
            out_specs=pl.BlockSpec(shape, lambda i, own, at: (0, 0, 0)),
        ),
        out_shape=jax.ShapeDtypeStruct(shape, jnp.bfloat16),
    )(owners, place, profiles, profiles, profiles, profiles, lengths)


def line_kernel(line_ref, out_ref):
    for i in range(0, NZ, 2):
        out_ref[i * FEATURES : (i + 2) * FEATURES, : 2 * WIDTH] = jnp.concatenate(
            [line_ref[i, :, : 2 * WIDTH], line_ref[i + 1, :, : 2 * WIDTH]], axis=0
        )
    lens = jnp.sum(line_ref[:, :, 2 * WIDTH :].astype(jnp.float32), axis=0)
    lens = jnp.concatenate([lens[:, :BLK], lens[:, BLK:], jnp.zeros((RUN - LENS, BLK), jnp.float32)], axis=0)
    out_ref[:, 2 * WIDTH :] = lens.astype(jnp.bfloat16)


def make_line(line):
    return pl.pallas_call(
        line_kernel,
        in_specs=[VMEM],
        out_specs=VMEM,
        out_shape=jax.ShapeDtypeStruct((RUN, 2 * WIDTH + BLK), jnp.bfloat16),
        compiler_params=params(6),
    )(line)


def group_kernel(a_ref, b_ref, c_ref, d_ref, mine_ref, other_ref):
    lens = jnp.zeros((LENS, BLK), jnp.float32)
    for i, ref in enumerate((a_ref, b_ref, c_ref, d_ref)):
        mine_ref[i * RUN : (i + 1) * RUN] = ref[:, :WIDTH]
        other_ref[i * RUN : (i + 1) * RUN] = ref[:, WIDTH : 2 * WIDTH]
        lens = lens + ref[:LENS, 2 * WIDTH :].astype(jnp.float32)
    mine_ref[GROUP:] = jnp.concatenate([lens] * (WIDTH // BLK), axis=1).astype(jnp.bfloat16)


def make_group(*blocks):
    return pl.pallas_call(
        group_kernel,
        in_specs=[VMEM] * 4,
        out_specs=[VMEM] * 2,
        out_shape=[
            jax.ShapeDtypeStruct((GROUP + LENS, WIDTH), jnp.bfloat16),
            jax.ShapeDtypeStruct((GROUP, WIDTH), jnp.bfloat16),
        ],
        compiler_params=params(6),
    )(*blocks)


def pack_kernel(*refs):
    panels, swapped, (own_ref, other_ref, len_ref) = refs[:4], refs[4:8], refs[8:]
    for i in range(4):
        own_ref[i * GROUP : (i + 1) * GROUP] = panels[i][:GROUP]
        other_ref[i * GROUP : (i + 1) * GROUP] = swapped[i][...]
    lens = sum(ref[GROUP:, :BLK].astype(jnp.float32) for ref in panels)
    lens = lens[:8] * 256 + lens[8:]
    len_ref[...] = jnp.concatenate([lens[j : j + 1] for j in range(8)], axis=1)


def pack(panels, swapped):
    whole = jax.ShapeDtypeStruct((4 * GROUP, WIDTH), jnp.bfloat16)
    return pl.pallas_call(
        pack_kernel,
        in_specs=[VMEM] * 8,
        out_specs=[VMEM] * 3,
        out_shape=[whole, whole, jax.ShapeDtypeStruct((1, WIDTH), jnp.float32)],
        compiler_params=params(6),
    )(*panels, *swapped)


def product(at_ref, rows_ref, panel_ref, x_inside, columns):
    y, x = at_ref[2], at_ref[3]
    parts = []
    for outer in range(4):
        for inner in range(4):
            ry = jnp.where(x_inside, outer, inner)
            rx = jnp.where(x_inside, inner, outer)
            source = jnp.bitwise_and(y - ry, NY - 1) * NX + jnp.bitwise_and(x - rx, NX - 1)
            parts.append(rows_ref[pl.ds(pl.multiple_of(source * RUN, RUN), RUN), columns])
    rows = jnp.concatenate(parts, axis=0)
    return lax.dot_general(rows, panel_ref[...], CONTRACT, preferred_element_type=jnp.float32)


def first_kernel(at_ref, rows_ref, panel_ref, out_ref):
    for i in range(PANEL // ROWS):
        columns = slice(i * ROWS, (i + 1) * ROWS)
        out_ref[columns, :] = product(at_ref, rows_ref, panel_ref, at_ref[1] == 0, columns)


def first_dot(place, local, panel):
    return pl.pallas_call(
        first_kernel,
        in_specs=[SMEM] + [VMEM] * 2,
        out_specs=VMEM,
        out_shape=jax.ShapeDtypeStruct((PANEL, WIDTH), jnp.float32),
        compiler_params=params(20),
        cost_estimate=pl.CostEstimate(flops=2 << 30, bytes_accessed=8 << 20, transcendentals=0),
    )(place, local, panel)


def second_kernel(
    at_ref, rows_ref, panel_ref, total_ref, col_len_ref, len_ref, mask_ref, out_ref, ready, sems
):
    left = at_ref[1] == 0
    col_len = col_len_ref[...]
    row_lens = len_ref[...].astype(jnp.float32).T
    side = HALF // BLK
    mask = jnp.concatenate(
        [jnp.where(left, mask_ref[t, :, :side], mask_ref[t, :, side:]) for t in range(SECTIONS)], axis=1
    ).astype(jnp.float32)
    row = lax.broadcasted_iota(jnp.int32, (2 * BLK, 2 * BLK), 0)
    column = lax.broadcasted_iota(jnp.int32, (2 * BLK, 2 * BLK), 1)
    at = jnp.bitwise_and(row, 1) * BLK + jnp.right_shift(row, 1)
    order = (column == at).astype(jnp.float32).astype(jnp.bfloat16)
    copies = []
    for i in range(PANEL // ROWS):
        columns = slice(i * ROWS, (i + 1) * ROWS)
        raw = product(at_ref, rows_ref, panel_ref, at_ref[1] == 1, columns) + total_ref[columns, :]
        for h in range(ROWS // BLK):
            b = i * (ROWS // BLK) + h
            norm = SCALE * lax.rsqrt(row_lens[:, b : b + 1] * col_len)
            spread = jnp.concatenate(
                [jnp.broadcast_to(mask[b : b + 1, j : j + 1], (BLK, BLK)) for j in range(WIDTH // BLK)], axis=1
            )
            scores = (raw[h * BLK : (h + 1) * BLK] * norm * spread).astype(jnp.bfloat16)
            stacked = jnp.concatenate([scores[:, :HALF], scores[:, HALF:]], axis=0)
            mixed = jnp.dot(order, stacked, preferred_element_type=jnp.float32).astype(jnp.bfloat16)
            ready[b * BLK : (b + 1) * BLK] = mixed.reshape(BLK, SECTIONS, HALF)
        copy = pltpu.make_async_copy(ready.at[columns], out_ref.at[columns], sems.at[i])
        copy.start()
        copies.append(copy)
    for copy in copies:
        copy.wait()


def second_dot(place, remote, panel, total, col_len, lengths, mask):
    return pl.pallas_call(
        second_kernel,
        in_specs=[SMEM] + [VMEM] * 6,
        out_specs=pl.BlockSpec(memory_space=pl.ANY),
        out_shape=jax.ShapeDtypeStruct((PANEL, SECTIONS, HALF), jnp.bfloat16),
        scratch_shapes=[
            pltpu.VMEM((PANEL, SECTIONS, HALF), jnp.bfloat16),
            pltpu.SemaphoreType.DMA((PANEL // ROWS,)),
        ],
        compiler_params=params(20),
        cost_estimate=pl.CostEstimate(flops=2 << 30, bytes_accessed=8 << 20, transcendentals=0),
    )(place, remote, panel, total, col_len, lengths, mask)


def shards(profiles, lengths, owners, block_mask):
    part = lax.axis_index("kmer")
    seq = lax.axis_index("seq")
    y, x = seq // (NX * NZ), seq // NZ % NX
    place = jnp.stack([seq, part, y, x]).astype(jnp.int32)
    piece = make_piece(owners, place, profiles, lengths)
    line = lax.all_to_all(piece, "seq", 0, 0, axis_index_groups=LINES, tiled=True)
    line, profiles = lax.optimization_barrier((line, profiles))
    local = lax.all_to_all(profiles, "seq", split_axis=1, concat_axis=0, tiled=True)

    line = make_line(line)
    mine, other = make_group(line, *[shift(line, 0, by) for by in (1, 2, 3)])
    mine_up, other_down = shift(mine, 1, 1), shift(other, 1, -1)
    other_up, mine_down = shift(other, 1, 1), shift(mine, 1, -1)
    mine_far, other_far = shift(mine_up, 1, 1), shift(other_down, 1, -1)
    panels = [mine, mine_up, mine_far, mine_down]
    swapped = [swap(a) for a in (other, other_up, other_far, other_down)]
    own_panel, other_panel, col_len = pack(panels, swapped)
    local, own_panel, other_panel, col_len = lax.optimization_barrier((local, own_panel, other_panel, col_len))
    remote = swap(local)
    total = first_dot(place, local, own_panel)
    return second_dot(place, remote, other_panel, total, col_len, lengths.reshape(PANEL // BLK, BLK), block_mask)


def solution(mesh):
    placed = (P(("seq", "kmer"), None), P("seq"), P(), P(None, "seq", None))
    return jax.shard_map(
        shards, mesh=mesh, in_specs=placed, out_specs=P("seq", None, "kmer"), check_vma=False
    )
```

```python
import jax
import jax.numpy as jnp
from jax import lax
from jax.experimental import pallas as pl
from jax.experimental.pallas import tpu as pltpu
from jax.sharding import PartitionSpec as P

KM = 2048
PANEL = 1024
BLK = 128
SECTIONS = 2
HALF = PANEL // 2
WIDTH = SECTIONS * HALF
SWAP = [(0, 1), (1, 0)]
NY, NX, NZ = 4, 4, 8
LINES = [[yx * NZ + z for z in range(NZ)] for yx in range(NY * NX)]
FEATURES = 8
RUN = NZ * FEATURES
GROUP = 4 * RUN
LENS = 16
SCALE = 256.0 / KM**0.5
ROWS = 256
VMEM = pl.BlockSpec(memory_space=pltpu.VMEM)
SMEM = pl.BlockSpec(memory_space=pltpu.SMEM)
CONTRACT = (((0,), (0,)), ((), ()))


def params(mebibytes):
    return pltpu.CompilerParams(vmem_limit_bytes=mebibytes << 20)


def number(y, x, z):
    return (y % NY * NX + x % NX) * NZ + z


def shift(value, turn, by):
    pairs = []
    for y in range(NY):
        for x in range(NX):
            for z in range(NZ):
                for core in range(2):
                    to = number(y, x + by, z) if core == turn else number(y + by, x, z)
                    pairs.append((number(y, x, z) * 2 + core, to * 2 + core))
    return lax.ppermute(value, ("seq", "kmer"), pairs)


def swap(value):
    return lax.ppermute(value, "kmer", SWAP)


def piece_kernel(own_ref, place_ref, a_ref, b_ref, c_ref, d_ref, len_ref, out_ref):
    seq = place_ref[0]
    for i, ref in enumerate((a_ref, b_ref, c_ref, d_ref)):
        out_ref[:, :, i * HALF : (i + 1) * HALF] = jnp.broadcast_to(ref[...][None], (NZ, FEATURES, HALF))
    size = len_ref[...].reshape(1, HALF)
    rows = [jnp.where(own_ref[t] == seq, size, 0) for t in range(SECTIONS)]
    for i in range(2):
        parts = []
        for t in range(SECTIONS):
            value = jnp.right_shift(rows[t], 8) if i == 0 else jnp.bitwise_and(rows[t], 255)
            value = value.astype(jnp.float32)
            parts += [value[:, j * BLK : (j + 1) * BLK] for j in range(HALF // BLK)]
        tile = jnp.concatenate(parts, axis=0).astype(jnp.bfloat16)
        at = 2 * WIDTH + i * BLK
        out_ref[:, :, at : at + BLK] = jnp.broadcast_to(tile[None], (NZ, FEATURES, BLK))


def make_piece(owners, place, profiles, lengths):
    def spec(t, other):
        def index(i, own, at):
            return 0, own[t] * 2 + (1 - at[1] if other else at[1])

        return pl.BlockSpec((FEATURES, HALF), index)

    shape = (NZ, FEATURES, 2 * WIDTH + 2 * BLK)
    return pl.pallas_call(
        piece_kernel,
        grid_spec=pltpu.PrefetchScalarGridSpec(
            num_scalar_prefetch=2,
            grid=(1,),
            in_specs=[
                spec(0, False),
                spec(1, False),
                spec(0, True),
                spec(1, True),
                pl.BlockSpec((HALF,), lambda i, own, at: (at[1],)),
            ],
            out_specs=pl.BlockSpec(shape, lambda i, own, at: (0, 0, 0)),
        ),
        out_shape=jax.ShapeDtypeStruct(shape, jnp.bfloat16),
    )(owners, place, profiles, profiles, profiles, profiles, lengths)


def line_kernel(line_ref, out_ref):
    for i in range(0, NZ, 2):
        out_ref[i * FEATURES : (i + 2) * FEATURES, : 2 * WIDTH] = jnp.concatenate(
            [line_ref[i, :, : 2 * WIDTH], line_ref[i + 1, :, : 2 * WIDTH]], axis=0
        )
    lens = jnp.sum(line_ref[:, :, 2 * WIDTH :].astype(jnp.float32), axis=0)
    lens = jnp.concatenate([lens[:, :BLK], lens[:, BLK:], jnp.zeros((RUN - LENS, BLK), jnp.float32)], axis=0)
    out_ref[:, 2 * WIDTH :] = lens.astype(jnp.bfloat16)


def make_line(line):
    return pl.pallas_call(
        line_kernel,
        in_specs=[VMEM],
        out_specs=VMEM,
        out_shape=jax.ShapeDtypeStruct((RUN, 2 * WIDTH + BLK), jnp.bfloat16),
        compiler_params=params(6),
    )(line)


def group_kernel(a_ref, b_ref, c_ref, d_ref, mine_ref, other_ref):
    lens = jnp.zeros((LENS, BLK), jnp.float32)
    for i, ref in enumerate((a_ref, b_ref, c_ref, d_ref)):
        mine_ref[i * RUN : (i + 1) * RUN] = ref[:, :WIDTH]
        other_ref[i * RUN : (i + 1) * RUN] = ref[:, WIDTH : 2 * WIDTH]
        lens = lens + ref[:LENS, 2 * WIDTH :].astype(jnp.float32)
    mine_ref[GROUP:] = jnp.concatenate([lens] * (WIDTH // BLK), axis=1).astype(jnp.bfloat16)


def make_group(*blocks):
    return pl.pallas_call(
        group_kernel,
        in_specs=[VMEM] * 4,
        out_specs=[VMEM] * 2,
        out_shape=[
            jax.ShapeDtypeStruct((GROUP + LENS, WIDTH), jnp.bfloat16),
            jax.ShapeDtypeStruct((GROUP, WIDTH), jnp.bfloat16),
        ],
        compiler_params=params(6),
    )(*blocks)


def pack_kernel(*refs):
    panels, swapped, (near_ref, rest_ref, other_ref, len_ref) = refs[:4], refs[4:8], refs[8:]
    for i in range(2):
        near_ref[i * GROUP : (i + 1) * GROUP] = panels[i][:GROUP]
        rest_ref[i * GROUP : (i + 1) * GROUP] = panels[2 + i][:GROUP]
    for i in range(4):
        other_ref[i * GROUP : (i + 1) * GROUP] = swapped[i][...]
    lens = sum(ref[GROUP:, :BLK].astype(jnp.float32) for ref in panels)
    lens = lens[:8] * 256 + lens[8:]
    len_ref[...] = jnp.concatenate([lens[j : j + 1] for j in range(8)], axis=1)


def pack(panels, swapped):
    return pl.pallas_call(
        pack_kernel,
        in_specs=[VMEM] * 8,
        out_specs=[VMEM] * 4,
        out_shape=[
            jax.ShapeDtypeStruct((2 * GROUP, WIDTH), jnp.bfloat16),
            jax.ShapeDtypeStruct((2 * GROUP, WIDTH), jnp.bfloat16),
            jax.ShapeDtypeStruct((4 * GROUP, WIDTH), jnp.bfloat16),
            jax.ShapeDtypeStruct((1, WIDTH), jnp.float32),
        ],
        compiler_params=params(6),
    )(*panels, *swapped)


def product(at_ref, rows_ref, panels, x_inside, columns):
    y, x = at_ref[2], at_ref[3]
    parts = []
    for outer in range(4):
        for inner in range(4):
            ry = jnp.where(x_inside, outer, inner)
            rx = jnp.where(x_inside, inner, outer)
            source = jnp.bitwise_and(y - ry, NY - 1) * NX + jnp.bitwise_and(x - rx, NX - 1)
            parts.append(rows_ref[pl.ds(pl.multiple_of(source * RUN, RUN), RUN), columns])
    rows = jnp.concatenate(parts, axis=0)
    panel = panels[0][...] if len(panels) == 1 else jnp.concatenate([p[...] for p in panels], axis=0)
    return lax.dot_general(rows, panel, CONTRACT, preferred_element_type=jnp.float32)


def first_kernel(at_ref, rows_ref, near_ref, rest_ref, out_ref):
    for i in range(PANEL // ROWS):
        columns = slice(i * ROWS, (i + 1) * ROWS)
        out_ref[columns, :] = product(at_ref, rows_ref, (near_ref, rest_ref), at_ref[1] == 0, columns)


def first_dot(place, local, near, rest):
    return pl.pallas_call(
        first_kernel,
        in_specs=[SMEM] + [VMEM] * 3,
        out_specs=VMEM,
        out_shape=jax.ShapeDtypeStruct((PANEL, WIDTH), jnp.float32),
        compiler_params=params(20),
        cost_estimate=pl.CostEstimate(flops=2 << 30, bytes_accessed=8 << 20, transcendentals=0),
    )(place, local, near, rest)


def second_kernel(
    at_ref, rows_ref, panel_ref, total_ref, col_len_ref, len_ref, mask_ref, out_ref, ready, sems
):
    left = at_ref[1] == 0
    col_len = col_len_ref[...]
    row_lens = len_ref[...].astype(jnp.float32).T
    side = HALF // BLK
    mask = jnp.concatenate(
        [jnp.where(left, mask_ref[t, :, :side], mask_ref[t, :, side:]) for t in range(SECTIONS)], axis=1
    ).astype(jnp.float32)
    row = lax.broadcasted_iota(jnp.int32, (2 * BLK, 2 * BLK), 0)
    column = lax.broadcasted_iota(jnp.int32, (2 * BLK, 2 * BLK), 1)
    at = jnp.bitwise_and(row, 1) * BLK + jnp.right_shift(row, 1)
    order = (column == at).astype(jnp.float32).astype(jnp.bfloat16)
    copies = []
    for i in range(PANEL // ROWS):
        columns = slice(i * ROWS, (i + 1) * ROWS)
        raw = product(at_ref, rows_ref, (panel_ref,), at_ref[1] == 1, columns) + total_ref[columns, :]
        for h in range(ROWS // BLK):
            b = i * (ROWS // BLK) + h
            norm = SCALE * lax.rsqrt(row_lens[:, b : b + 1] * col_len)
            spread = jnp.concatenate(
                [jnp.broadcast_to(mask[b : b + 1, j : j + 1], (BLK, BLK)) for j in range(WIDTH // BLK)], axis=1
            )
            scores = (raw[h * BLK : (h + 1) * BLK] * norm * spread).astype(jnp.bfloat16)
            stacked = jnp.concatenate([scores[:, :HALF], scores[:, HALF:]], axis=0)
            mixed = jnp.dot(order, stacked, preferred_element_type=jnp.float32).astype(jnp.bfloat16)
            ready[b * BLK : (b + 1) * BLK] = mixed.reshape(BLK, SECTIONS, HALF)
        copy = pltpu.make_async_copy(ready.at[columns], out_ref.at[columns], sems.at[i])
        copy.start()
        copies.append(copy)
    for copy in copies:
        copy.wait()


def second_dot(place, remote, panel, total, col_len, lengths, mask):
    return pl.pallas_call(
        second_kernel,
        in_specs=[SMEM] + [VMEM] * 6,
        out_specs=pl.BlockSpec(memory_space=pl.ANY),
        out_shape=jax.ShapeDtypeStruct((PANEL, SECTIONS, HALF), jnp.bfloat16),
        scratch_shapes=[
            pltpu.VMEM((PANEL, SECTIONS, HALF), jnp.bfloat16),
            pltpu.SemaphoreType.DMA((PANEL // ROWS,)),
        ],
        compiler_params=params(20),
        cost_estimate=pl.CostEstimate(flops=2 << 30, bytes_accessed=8 << 20, transcendentals=0),
    )(place, remote, panel, total, col_len, lengths, mask)


def shards(profiles, lengths, owners, block_mask):
    part = lax.axis_index("kmer")
    seq = lax.axis_index("seq")
    y, x = seq // (NX * NZ), seq // NZ % NX
    place = jnp.stack([seq, part, y, x]).astype(jnp.int32)
    piece = make_piece(owners, place, profiles, lengths)
    line = lax.all_to_all(piece, "seq", 0, 0, axis_index_groups=LINES, tiled=True)
    line, profiles = lax.optimization_barrier((line, profiles))
    local = lax.all_to_all(profiles, "seq", split_axis=1, concat_axis=0, tiled=True)

    line = make_line(line)
    mine, other = make_group(line, *[shift(line, 0, by) for by in (1, 2, 3)])
    mine_up, other_down = shift(mine, 1, 1), shift(other, 1, -1)
    other_up, mine_down = shift(other, 1, 1), shift(mine, 1, -1)
    mine_far, other_far = shift(mine_up, 1, 1), shift(other_down, 1, -1)
    panels = [mine, mine_up, mine_far, mine_down]
    swapped = [swap(a) for a in (other, other_up, other_far, other_down)]
    near, rest, other_panel, col_len = pack(panels, swapped)
    local, near, rest, other_panel, col_len = lax.optimization_barrier((local, near, rest, other_panel, col_len))
    remote = swap(local)
    total = first_dot(place, local, near, rest)
    return second_dot(place, remote, other_panel, total, col_len, lengths.reshape(PANEL // BLK, BLK), block_mask)


def solution(mesh):
    placed = (P(("seq", "kmer"), None), P("seq"), P(), P(None, "seq", None))
    return jax.shard_map(
        shards, mesh=mesh, in_specs=placed, out_specs=P("seq", None, "kmer"), check_vma=False
    )
```

```python
import jax
import jax.numpy as jnp
from jax import lax
from jax.experimental import pallas as pl
from jax.experimental.pallas import tpu as pltpu
from jax.sharding import PartitionSpec as P

KM = 2048
PANEL = 1024
BLK = 128
SECTIONS = 2
HALF = PANEL // 2
WIDTH = SECTIONS * HALF
SWAP = [(0, 1), (1, 0)]
NY, NX, NZ = 4, 4, 8
LINES = [[yx * NZ + z for z in range(NZ)] for yx in range(NY * NX)]
FEATURES = 8
RUN = NZ * FEATURES
GROUP = 4 * RUN
LENS = 16
SCALE = 256.0 / KM**0.5
ROWS = 256
VMEM = pl.BlockSpec(memory_space=pltpu.VMEM)
SMEM = pl.BlockSpec(memory_space=pltpu.SMEM)
CONTRACT = (((0,), (0,)), ((), ()))


def params(mebibytes):
    return pltpu.CompilerParams(vmem_limit_bytes=mebibytes << 20)


def number(y, x, z):
    return (y % NY * NX + x % NX) * NZ + z


def shift(value, turn, by):
    pairs = []
    for y in range(NY):
        for x in range(NX):
            for z in range(NZ):
                for core in range(2):
                    to = number(y, x + by, z) if core == turn else number(y + by, x, z)
                    pairs.append((number(y, x, z) * 2 + core, to * 2 + core))
    return lax.ppermute(value, ("seq", "kmer"), pairs)


def swap(value):
    return lax.ppermute(value, "kmer", SWAP)


def piece_kernel(own_ref, place_ref, a_ref, b_ref, c_ref, d_ref, len_ref, out_ref):
    seq = place_ref[0]
    for i, ref in enumerate((a_ref, b_ref, c_ref, d_ref)):
        out_ref[:, :, i * HALF : (i + 1) * HALF] = jnp.broadcast_to(ref[...][None], (NZ, FEATURES, HALF))
    size = len_ref[...].reshape(1, HALF)
    rows = [jnp.where(own_ref[t] == seq, size, 0) for t in range(SECTIONS)]
    for i in range(2):
        parts = []
        for t in range(SECTIONS):
            value = jnp.right_shift(rows[t], 8) if i == 0 else jnp.bitwise_and(rows[t], 255)
            value = value.astype(jnp.float32)
            parts += [value[:, j * BLK : (j + 1) * BLK] for j in range(HALF // BLK)]
        tile = jnp.concatenate(parts, axis=0).astype(jnp.bfloat16)
        at = 2 * WIDTH + i * BLK
        out_ref[:, :, at : at + BLK] = jnp.broadcast_to(tile[None], (NZ, FEATURES, BLK))


def make_piece(owners, place, profiles, lengths):
    def spec(t, other):
        def index(i, own, at):
            return 0, own[t] * 2 + (1 - at[1] if other else at[1])

        return pl.BlockSpec((FEATURES, HALF), index)

    shape = (NZ, FEATURES, 2 * WIDTH + 2 * BLK)
    return pl.pallas_call(
        piece_kernel,
        grid_spec=pltpu.PrefetchScalarGridSpec(
            num_scalar_prefetch=2,
            grid=(1,),
            in_specs=[
                spec(0, False),
                spec(1, False),
                spec(0, True),
                spec(1, True),
                pl.BlockSpec((HALF,), lambda i, own, at: (at[1],)),
            ],
            out_specs=pl.BlockSpec(shape, lambda i, own, at: (0, 0, 0)),
        ),
        out_shape=jax.ShapeDtypeStruct(shape, jnp.bfloat16),
    )(owners, place, profiles, profiles, profiles, profiles, lengths)


def line_kernel(line_ref, out_ref):
    for i in range(0, NZ, 2):
        out_ref[i * FEATURES : (i + 2) * FEATURES, : 2 * WIDTH] = jnp.concatenate(
            [line_ref[i, :, : 2 * WIDTH], line_ref[i + 1, :, : 2 * WIDTH]], axis=0
        )
    lens = jnp.sum(line_ref[:, :, 2 * WIDTH :].astype(jnp.float32), axis=0)
    lens = jnp.concatenate([lens[:, :BLK], lens[:, BLK:], jnp.zeros((RUN - LENS, BLK), jnp.float32)], axis=0)
    out_ref[:, 2 * WIDTH :] = lens.astype(jnp.bfloat16)


def make_line(line):
    return pl.pallas_call(
        line_kernel,
        in_specs=[VMEM],
        out_specs=VMEM,
        out_shape=jax.ShapeDtypeStruct((RUN, 2 * WIDTH + BLK), jnp.bfloat16),
        compiler_params=params(6),
    )(line)


def group_kernel(a_ref, b_ref, c_ref, d_ref, mine_ref, other_ref):
    lens = jnp.zeros((LENS, BLK), jnp.float32)
    for i, ref in enumerate((a_ref, b_ref, c_ref, d_ref)):
        mine_ref[i * RUN : (i + 1) * RUN] = ref[:, :WIDTH]
        other_ref[i * RUN : (i + 1) * RUN] = ref[:, WIDTH : 2 * WIDTH]
        lens = lens + ref[:LENS, 2 * WIDTH :].astype(jnp.float32)
    mine_ref[GROUP:] = jnp.concatenate([lens] * (WIDTH // BLK), axis=1).astype(jnp.bfloat16)


def make_group(*blocks):
    return pl.pallas_call(
        group_kernel,
        in_specs=[VMEM] * 4,
        out_specs=[VMEM] * 2,
        out_shape=[
            jax.ShapeDtypeStruct((GROUP + LENS, WIDTH), jnp.bfloat16),
            jax.ShapeDtypeStruct((GROUP, WIDTH), jnp.bfloat16),
        ],
        compiler_params=params(6),
    )(*blocks)


def pack_kernel(*refs):
    blocks, out_ref = refs[:-1], refs[-1]
    for i, ref in enumerate(blocks):
        out_ref[i * GROUP : (i + 1) * GROUP] = ref[:GROUP]


def pack(*blocks):
    return pl.pallas_call(
        pack_kernel,
        in_specs=[VMEM] * len(blocks),
        out_specs=VMEM,
        out_shape=jax.ShapeDtypeStruct((len(blocks) * GROUP, WIDTH), jnp.bfloat16),
        compiler_params=params(6),
    )(*blocks)


def pack_last_kernel(*refs):
    panels, (rest_ref, len_ref) = refs[:4], refs[4:]
    for i in range(2):
        rest_ref[i * GROUP : (i + 1) * GROUP] = panels[2 + i][:GROUP]
    lens = sum(ref[GROUP:, :BLK].astype(jnp.float32) for ref in panels)
    lens = lens[:8] * 256 + lens[8:]
    len_ref[...] = jnp.concatenate([lens[j : j + 1] for j in range(8)], axis=1)


def pack_last(*panels):
    return pl.pallas_call(
        pack_last_kernel,
        in_specs=[VMEM] * 4,
        out_specs=[VMEM] * 2,
        out_shape=[
            jax.ShapeDtypeStruct((2 * GROUP, WIDTH), jnp.bfloat16),
            jax.ShapeDtypeStruct((1, WIDTH), jnp.float32),
        ],
        compiler_params=params(6),
    )(*panels)


def product(at_ref, rows_ref, panels, x_inside, columns):
    y, x = at_ref[2], at_ref[3]
    parts = []
    for outer in range(4):
        for inner in range(4):
            ry = jnp.where(x_inside, outer, inner)
            rx = jnp.where(x_inside, inner, outer)
            source = jnp.bitwise_and(y - ry, NY - 1) * NX + jnp.bitwise_and(x - rx, NX - 1)
            parts.append(rows_ref[pl.ds(pl.multiple_of(source * RUN, RUN), RUN), columns])
    rows = jnp.concatenate(parts, axis=0)
    panel = panels[0][...] if len(panels) == 1 else jnp.concatenate([p[...] for p in panels], axis=0)
    return lax.dot_general(rows, panel, CONTRACT, preferred_element_type=jnp.float32)


def first_kernel(at_ref, rows_ref, near_ref, rest_ref, out_ref):
    for i in range(PANEL // ROWS):
        columns = slice(i * ROWS, (i + 1) * ROWS)
        out_ref[columns, :] = product(at_ref, rows_ref, (near_ref, rest_ref), at_ref[1] == 0, columns)


def first_dot(place, local, near, rest):
    return pl.pallas_call(
        first_kernel,
        in_specs=[SMEM] + [VMEM] * 3,
        out_specs=VMEM,
        out_shape=jax.ShapeDtypeStruct((PANEL, WIDTH), jnp.float32),
        compiler_params=params(20),
        cost_estimate=pl.CostEstimate(flops=2 << 30, bytes_accessed=8 << 20, transcendentals=0),
    )(place, local, near, rest)


def second_kernel(
    at_ref, rows_ref, panel_ref, total_ref, col_len_ref, len_ref, mask_ref, out_ref, ready, sems
):
    left = at_ref[1] == 0
    col_len = col_len_ref[...]
    row_lens = len_ref[...].astype(jnp.float32).T
    side = HALF // BLK
    mask = jnp.concatenate(
        [jnp.where(left, mask_ref[t, :, :side], mask_ref[t, :, side:]) for t in range(SECTIONS)], axis=1
    ).astype(jnp.float32)
    row = lax.broadcasted_iota(jnp.int32, (2 * BLK, 2 * BLK), 0)
    column = lax.broadcasted_iota(jnp.int32, (2 * BLK, 2 * BLK), 1)
    at = jnp.bitwise_and(row, 1) * BLK + jnp.right_shift(row, 1)
    order = (column == at).astype(jnp.float32).astype(jnp.bfloat16)
    copies = []
    for i in range(PANEL // ROWS):
        columns = slice(i * ROWS, (i + 1) * ROWS)
        raw = product(at_ref, rows_ref, (panel_ref,), at_ref[1] == 1, columns) + total_ref[columns, :]
        for h in range(ROWS // BLK):
            b = i * (ROWS // BLK) + h
            norm = SCALE * lax.rsqrt(row_lens[:, b : b + 1] * col_len)
            spread = jnp.concatenate(
                [jnp.broadcast_to(mask[b : b + 1, j : j + 1], (BLK, BLK)) for j in range(WIDTH // BLK)], axis=1
            )
            scores = (raw[h * BLK : (h + 1) * BLK] * norm * spread).astype(jnp.bfloat16)
            stacked = jnp.concatenate([scores[:, :HALF], scores[:, HALF:]], axis=0)
            mixed = jnp.dot(order, stacked, preferred_element_type=jnp.float32).astype(jnp.bfloat16)
            ready[b * BLK : (b + 1) * BLK] = mixed.reshape(BLK, SECTIONS, HALF)
        copy = pltpu.make_async_copy(ready.at[columns], out_ref.at[columns], sems.at[i])
        copy.start()
        copies.append(copy)
    for copy in copies:
        copy.wait()


def second_dot(place, remote, panel, total, col_len, lengths, mask):
    return pl.pallas_call(
        second_kernel,
        in_specs=[SMEM] + [VMEM] * 6,
        out_specs=pl.BlockSpec(memory_space=pl.ANY),
        out_shape=jax.ShapeDtypeStruct((PANEL, SECTIONS, HALF), jnp.bfloat16),
        scratch_shapes=[
            pltpu.VMEM((PANEL, SECTIONS, HALF), jnp.bfloat16),
            pltpu.SemaphoreType.DMA((PANEL // ROWS,)),
        ],
        compiler_params=params(20),
        cost_estimate=pl.CostEstimate(flops=2 << 30, bytes_accessed=8 << 20, transcendentals=0),
    )(place, remote, panel, total, col_len, lengths, mask)


def shards(profiles, lengths, owners, block_mask):
    part = lax.axis_index("kmer")
    seq = lax.axis_index("seq")
    y, x = seq // (NX * NZ), seq // NZ % NX
    place = jnp.stack([seq, part, y, x]).astype(jnp.int32)
    piece = make_piece(owners, place, profiles, lengths)
    line = lax.all_to_all(piece, "seq", 0, 0, axis_index_groups=LINES, tiled=True)
    line, profiles = lax.optimization_barrier((line, profiles))
    local = lax.all_to_all(profiles, "seq", split_axis=1, concat_axis=0, tiled=True)

    line = make_line(line)
    mine, other = make_group(line, *[shift(line, 0, by) for by in (1, 2, 3)])
    mine_up, other_down = shift(mine, 1, 1), shift(other, 1, -1)
    other_up, mine_down = shift(other, 1, 1), shift(mine, 1, -1)
    mine_far, other_far = shift(mine_up, 1, 1), shift(other_down, 1, -1)
    panels = [mine, mine_up, mine_far, mine_down]
    swapped = [swap(a) for a in (other, other_up, other_far, other_down)]
    near = pack(*panels[:2])
    other_panel = pack(*swapped)
    panels[3], other_panel = lax.optimization_barrier((panels[3], other_panel))
    rest, col_len = pack_last(*panels)
    local, near, rest, other_panel, col_len = lax.optimization_barrier((local, near, rest, other_panel, col_len))
    remote = swap(local)
    total = first_dot(place, local, near, rest)
    return second_dot(place, remote, other_panel, total, col_len, lengths.reshape(PANEL // BLK, BLK), block_mask)


def solution(mesh):
    placed = (P(("seq", "kmer"), None), P("seq"), P(), P(None, "seq", None))
    return jax.shard_map(
        shards, mesh=mesh, in_specs=placed, out_specs=P("seq", None, "kmer"), check_vma=False
    )
```

```python
import jax
import jax.numpy as jnp
from jax import lax
from jax.experimental import pallas as pl
from jax.experimental.pallas import tpu as pltpu
from jax.sharding import PartitionSpec as P

KM = 2048
PANEL = 1024
BLK = 128
SECTIONS = 2
HALF = PANEL // 2
WIDTH = SECTIONS * HALF
SWAP = [(0, 1), (1, 0)]
NY, NX, NZ = 4, 4, 8
LINES = [[yx * NZ + z for z in range(NZ)] for yx in range(NY * NX)]
FEATURES = 8
RUN = NZ * FEATURES
GROUP = 4 * RUN
LENS = 16
SCALE = 256.0 / KM**0.5
ROWS = 256
VMEM = pl.BlockSpec(memory_space=pltpu.VMEM)
SMEM = pl.BlockSpec(memory_space=pltpu.SMEM)
CONTRACT = (((0,), (0,)), ((), ()))


def params(mebibytes):
    return pltpu.CompilerParams(vmem_limit_bytes=mebibytes << 20)


def number(y, x, z):
    return (y % NY * NX + x % NX) * NZ + z


def shift(value, turn, by):
    pairs = []
    for y in range(NY):
        for x in range(NX):
            for z in range(NZ):
                for core in range(2):
                    to = number(y, x + by, z) if core == turn else number(y + by, x, z)
                    pairs.append((number(y, x, z) * 2 + core, to * 2 + core))
    return lax.ppermute(value, ("seq", "kmer"), pairs)


def swap(value):
    return lax.ppermute(value, "kmer", SWAP)


def piece_kernel(own_ref, place_ref, a_ref, b_ref, c_ref, d_ref, len_ref, out_ref):
    seq = place_ref[0]
    for i, ref in enumerate((a_ref, b_ref, c_ref, d_ref)):
        out_ref[:, :, i * HALF : (i + 1) * HALF] = jnp.broadcast_to(ref[...][None], (NZ, FEATURES, HALF))
    size = len_ref[...].reshape(1, HALF)
    rows = [jnp.where(own_ref[t] == seq, size, 0) for t in range(SECTIONS)]
    for i in range(2):
        parts = []
        for t in range(SECTIONS):
            value = jnp.right_shift(rows[t], 8) if i == 0 else jnp.bitwise_and(rows[t], 255)
            value = value.astype(jnp.float32)
            parts += [value[:, j * BLK : (j + 1) * BLK] for j in range(HALF // BLK)]
        tile = jnp.concatenate(parts, axis=0).astype(jnp.bfloat16)
        at = 2 * WIDTH + i * BLK
        out_ref[:, :, at : at + BLK] = jnp.broadcast_to(tile[None], (NZ, FEATURES, BLK))


def make_piece(owners, place, profiles, lengths):
    def spec(t, other):
        def index(i, own, at):
            return 0, own[t] * 2 + (1 - at[1] if other else at[1])

        return pl.BlockSpec((FEATURES, HALF), index)

    shape = (NZ, FEATURES, 2 * WIDTH + 2 * BLK)
    return pl.pallas_call(
        piece_kernel,
        grid_spec=pltpu.PrefetchScalarGridSpec(
            num_scalar_prefetch=2,
            grid=(1,),
            in_specs=[
                spec(0, False),
                spec(1, False),
                spec(0, True),
                spec(1, True),
                pl.BlockSpec((HALF,), lambda i, own, at: (at[1],)),
            ],
            out_specs=pl.BlockSpec(shape, lambda i, own, at: (0, 0, 0)),
        ),
        out_shape=jax.ShapeDtypeStruct(shape, jnp.bfloat16),
    )(owners, place, profiles, profiles, profiles, profiles, lengths)


def line_kernel(line_ref, out_ref):
    for i in range(0, NZ, 2):
        out_ref[i * FEATURES : (i + 2) * FEATURES, : 2 * WIDTH] = jnp.concatenate(
            [line_ref[i, :, : 2 * WIDTH], line_ref[i + 1, :, : 2 * WIDTH]], axis=0
        )
    lens = jnp.sum(line_ref[:, :, 2 * WIDTH :].astype(jnp.float32), axis=0)
    lens = jnp.concatenate([lens[:, :BLK], lens[:, BLK:], jnp.zeros((RUN - LENS, BLK), jnp.float32)], axis=0)
    out_ref[:, 2 * WIDTH :] = lens.astype(jnp.bfloat16)


def make_line(line):
    return pl.pallas_call(
        line_kernel,
        in_specs=[VMEM],
        out_specs=VMEM,
        out_shape=jax.ShapeDtypeStruct((RUN, 2 * WIDTH + BLK), jnp.bfloat16),
        compiler_params=params(6),
    )(line)


def group_kernel(a_ref, b_ref, c_ref, d_ref, mine_ref, other_ref):
    lens = jnp.zeros((LENS, BLK), jnp.float32)
    for i, ref in enumerate((a_ref, b_ref, c_ref, d_ref)):
        mine_ref[i * RUN : (i + 1) * RUN] = ref[:, :WIDTH]
        other_ref[i * RUN : (i + 1) * RUN] = ref[:, WIDTH : 2 * WIDTH]
        lens = lens + ref[:LENS, 2 * WIDTH :].astype(jnp.float32)
    mine_ref[GROUP:] = jnp.concatenate([lens] * (WIDTH // BLK), axis=1).astype(jnp.bfloat16)


def make_group(*blocks):
    return pl.pallas_call(
        group_kernel,
        in_specs=[VMEM] * 4,
        out_specs=[VMEM] * 2,
        out_shape=[
            jax.ShapeDtypeStruct((GROUP + LENS, WIDTH), jnp.bfloat16),
            jax.ShapeDtypeStruct((GROUP, WIDTH), jnp.bfloat16),
        ],
        compiler_params=params(6),
    )(*blocks)


def pack_kernel(*refs):
    blocks, out_ref = refs[:-1], refs[-1]
    for i, ref in enumerate(blocks):
        out_ref[i * GROUP : (i + 1) * GROUP] = ref[:GROUP]


def pack(*blocks):
    return pl.pallas_call(
        pack_kernel,
        in_specs=[VMEM] * len(blocks),
        out_specs=VMEM,
        out_shape=jax.ShapeDtypeStruct((len(blocks) * GROUP, WIDTH), jnp.bfloat16),
        compiler_params=params(6),
    )(*blocks)


def pack_last_kernel(*refs):
    panels, (rest_ref, len_ref) = refs[:4], refs[4:]
    rest_ref[...] = panels[2][:GROUP]
    lens = sum(ref[GROUP:, :BLK].astype(jnp.float32) for ref in panels)
    lens = lens[:8] * 256 + lens[8:]
    len_ref[...] = jnp.concatenate([lens[j : j + 1] for j in range(8)], axis=1)


def pack_last(*panels):
    return pl.pallas_call(
        pack_last_kernel,
        in_specs=[VMEM] * 4,
        out_specs=[VMEM] * 2,
        out_shape=[
            jax.ShapeDtypeStruct((GROUP, WIDTH), jnp.bfloat16),
            jax.ShapeDtypeStruct((1, WIDTH), jnp.float32),
        ],
        compiler_params=params(6),
    )(*panels)


def product(at_ref, rows_ref, panels, x_inside, columns):
    y, x = at_ref[2], at_ref[3]
    parts = []
    for outer in range(4):
        for inner in range(4):
            ry = jnp.where(x_inside, outer, inner)
            rx = jnp.where(x_inside, inner, outer)
            source = jnp.bitwise_and(y - ry, NY - 1) * NX + jnp.bitwise_and(x - rx, NX - 1)
            parts.append(rows_ref[pl.ds(pl.multiple_of(source * RUN, RUN), RUN), columns])
    rows = jnp.concatenate(parts, axis=0)
    panel = panels[0][...] if len(panels) == 1 else jnp.concatenate([p[...] for p in panels], axis=0)
    return lax.dot_general(rows, panel, CONTRACT, preferred_element_type=jnp.float32)


def first_kernel(at_ref, rows_ref, near_ref, rest_ref, out_ref):
    for i in range(PANEL // ROWS):
        columns = slice(i * ROWS, (i + 1) * ROWS)
        out_ref[columns, :] = product(at_ref, rows_ref, (near_ref.at[: 2 * GROUP], rest_ref, near_ref.at[2 * GROUP :]), at_ref[1] == 0, columns)


def first_dot(place, local, near, rest):
    return pl.pallas_call(
        first_kernel,
        in_specs=[SMEM] + [VMEM] * 3,
        out_specs=VMEM,
        out_shape=jax.ShapeDtypeStruct((PANEL, WIDTH), jnp.float32),
        compiler_params=params(20),
        cost_estimate=pl.CostEstimate(flops=2 << 30, bytes_accessed=8 << 20, transcendentals=0),
    )(place, local, near, rest)


def second_kernel(
    at_ref, rows_ref, panel_ref, total_ref, col_len_ref, len_ref, mask_ref, out_ref, ready, sems
):
    left = at_ref[1] == 0
    col_len = col_len_ref[...]
    row_lens = len_ref[...].astype(jnp.float32).T
    side = HALF // BLK
    mask = jnp.concatenate(
        [jnp.where(left, mask_ref[t, :, :side], mask_ref[t, :, side:]) for t in range(SECTIONS)], axis=1
    ).astype(jnp.float32)
    row = lax.broadcasted_iota(jnp.int32, (2 * BLK, 2 * BLK), 0)
    column = lax.broadcasted_iota(jnp.int32, (2 * BLK, 2 * BLK), 1)
    at = jnp.bitwise_and(row, 1) * BLK + jnp.right_shift(row, 1)
    order = (column == at).astype(jnp.float32).astype(jnp.bfloat16)
    copies = []
    for i in range(PANEL // ROWS):
        columns = slice(i * ROWS, (i + 1) * ROWS)
        raw = product(at_ref, rows_ref, (panel_ref,), at_ref[1] == 1, columns) + total_ref[columns, :]
        for h in range(ROWS // BLK):
            b = i * (ROWS // BLK) + h
            norm = SCALE * lax.rsqrt(row_lens[:, b : b + 1] * col_len)
            spread = jnp.concatenate(
                [jnp.broadcast_to(mask[b : b + 1, j : j + 1], (BLK, BLK)) for j in range(WIDTH // BLK)], axis=1
            )
            scores = (raw[h * BLK : (h + 1) * BLK] * norm * spread).astype(jnp.bfloat16)
            stacked = jnp.concatenate([scores[:, :HALF], scores[:, HALF:]], axis=0)
            mixed = jnp.dot(order, stacked, preferred_element_type=jnp.float32).astype(jnp.bfloat16)
            ready[b * BLK : (b + 1) * BLK] = mixed.reshape(BLK, SECTIONS, HALF)
        copy = pltpu.make_async_copy(ready.at[columns], out_ref.at[columns], sems.at[i])
        copy.start()
        copies.append(copy)
    for copy in copies:
        copy.wait()


def second_dot(place, remote, panel, total, col_len, lengths, mask):
    return pl.pallas_call(
        second_kernel,
        in_specs=[SMEM] + [VMEM] * 6,
        out_specs=pl.BlockSpec(memory_space=pl.ANY),
        out_shape=jax.ShapeDtypeStruct((PANEL, SECTIONS, HALF), jnp.bfloat16),
        scratch_shapes=[
            pltpu.VMEM((PANEL, SECTIONS, HALF), jnp.bfloat16),
            pltpu.SemaphoreType.DMA((PANEL // ROWS,)),
        ],
        compiler_params=params(20),
        cost_estimate=pl.CostEstimate(flops=2 << 30, bytes_accessed=8 << 20, transcendentals=0),
    )(place, remote, panel, total, col_len, lengths, mask)


def shards(profiles, lengths, owners, block_mask):
    part = lax.axis_index("kmer")
    seq = lax.axis_index("seq")
    y, x = seq // (NX * NZ), seq // NZ % NX
    place = jnp.stack([seq, part, y, x]).astype(jnp.int32)
    piece = make_piece(owners, place, profiles, lengths)
    line = lax.all_to_all(piece, "seq", 0, 0, axis_index_groups=LINES, tiled=True)
    line, profiles = lax.optimization_barrier((line, profiles))
    local = lax.all_to_all(profiles, "seq", split_axis=1, concat_axis=0, tiled=True)

    line = make_line(line)
    mine, other = make_group(line, *[shift(line, 0, by) for by in (1, 2, 3)])
    mine_up, other_down = shift(mine, 1, 1), shift(other, 1, -1)
    other_up, mine_down = shift(other, 1, 1), shift(mine, 1, -1)
    mine_far, other_far = shift(mine_up, 1, 1), shift(other_down, 1, -1)
    panels = [mine, mine_up, mine_far, mine_down]
    swapped = [swap(a) for a in (other, other_up, other_far, other_down)]
    near = pack(panels[0], panels[1], panels[3])
    other_panel = pack(*swapped)
    panels[2], other_panel, near = lax.optimization_barrier((panels[2], other_panel, near))
    rest, col_len = pack_last(*panels)
    local, near, rest, other_panel, col_len = lax.optimization_barrier((local, near, rest, other_panel, col_len))
    remote = swap(local)
    total = first_dot(place, local, near, rest)
    return second_dot(place, remote, other_panel, total, col_len, lengths.reshape(PANEL // BLK, BLK), block_mask)


def solution(mesh):
    placed = (P(("seq", "kmer"), None), P("seq"), P(), P(None, "seq", None))
    return jax.shard_map(
        shards, mesh=mesh, in_specs=placed, out_specs=P("seq", None, "kmer"), check_vma=False
    )
```
